32 devices in a mesh: row: 8 (over y, x, core), col: 4 (over z).
Axes of the slice: x: 2, y: 2, z: 4, core: 2. Of those that a mesh axis runs over, the one named last changes fastest.
Arguments:
- features: bfloat16 [4096, 512], P(('row', 'col')), may hold values from -6 to 6
- weight: bfloat16 [512, 512], replicated, may hold values from -0.25 to 0.25
- edge_tiles: bfloat16 [8, 4, 4, 3, 128, 128], P('row', 'col'), may hold values from -0.3125 to 0.3125
- tile_col: int32 [8, 4, 4, 3], P('row', 'col'), may hold values from 0 to 7, as said below
- tile_count: int32 [8, 4, 4], P('row', 'col'), may hold values from 0 to 3, as said below
- cotangent: bfloat16 [4096, 512], P(('row', 'col')), may hold values from -0.09375 to 0.09375
Outputs:
- activations: bfloat16 [4096, 512], P(('row', 'col'))
- weight_grad: float32 [512, 512], replicated
The draws below stay inside these ranges and needn't reach their ends.
Inputs may be any that keep to these rules, and one draw needn't show every extreme that they name: `tile_col`: the live slots of one row block name different column blocks; slots that are not live hold arbitrary column blocks. Slots 0 to tile_count - 1 of a row block are live; the others hold arbitrary edge weights that are not part of the adjacency. Some row block holds 3 live slots.
All inputs are finite; a program needn't handle non-finite values.
Results may differ from the reference program's by a relative error of at most 0.024.
Values may be sent and summed in bfloat16 or wider, within the bound.
No kernel may reach another device: no remote copies, remote signals or barrier semaphores. Data moves between devices by JAX's collectives and lax.ppermute only.
A program may use at most 64 MiB of HBM per device.

```python
import jax
import jax.numpy as jnp
from jax import lax

F = 512
H = 512
BLK = 128
KR = 3
RBLK = 4
CBLK = 8
NODES = 4096


def draw_tile_count(key, part):
    base = jax.random.fold_in(key, 11)
    key_level, key_pick, key_cut, key_top = jax.random.split(base, 4)
    level = jax.random.randint(key_level, (CBLK, RBLK, 1), 1, KR + 1)
    picked = jax.random.randint(key_pick, (), 0, CBLK * RBLK)
    device_ids = jnp.arange(CBLK * RBLK, dtype=jnp.int32).reshape(CBLK, RBLK, 1)
    level = jnp.where(device_ids == picked, KR, level)
    cut = jax.random.randint(key_cut, (CBLK, RBLK, RBLK), 0, 4)
    count = level - cut * level // 6
    top_block = jax.random.randint(key_top, (CBLK, RBLK, 1), 0, RBLK)
    block_ids = jnp.arange(RBLK, dtype=jnp.int32)[None, None, :]
    count = jnp.where(block_ids == top_block, level, count)
    return count.astype(jnp.int32)


def draw_tile_col(key, part):
    base = jax.random.fold_in(key, 23)
    scores = jax.random.randint(base, (CBLK, RBLK, RBLK, CBLK), 0, 1 << 20)
    scores = scores * CBLK + jnp.arange(CBLK, dtype=jnp.int32)
    order = jnp.argsort(scores, axis=-1)
    return order[..., :KR].astype(jnp.int32)


def with_spikes(drawn, stream_key, source, target, shards_of, factor):
    def block_of(axis_at):
        return (jnp.arange(drawn.shape[axis_at]) // (drawn.shape[axis_at] // shards_of)).reshape((-1,) + (1,) * (drawn.ndim - 1 - axis_at))

    one_side = jax.random.permutation(stream_key, shards_of)[block_of(target)]
    other_side = (block_of(target) + shards_of // 2) % shards_of
    return jnp.where((block_of(source) == one_side) | (block_of(source) == other_side), factor * drawn, drawn)


def levels(own_key, shape, shards, least, high):
    loudness, own = 1.0, jax.random.fold_in(own_key, 6)
    for dim, parts in shards:
        draws = jnp.exp(jax.random.uniform(jax.random.fold_in(own, dim), (parts,), jnp.float32, least / len(shards), high / len(shards)))
        loudness = loudness * jnp.repeat(draws, shape[dim] // parts).reshape([-1 if axis == dim else 1 for axis in range(len(shape))])
    return loudness


def scatter_about(own_key, extent, deviation, most, cuts=(), kind=jnp.bfloat16):
    result = deviation * jax.random.normal(own_key, extent, jnp.float32)
    if cuts:
        result = result * levels(own_key, extent, cuts, -0.22, 0.18)
    return jnp.clip(result, -most, most).astype(kind)


def noise_with(key, dims, scale, bound, pieces, heavy, kind=jnp.bfloat16):
    result = scale * jax.random.normal(key, dims, jnp.float32)
    if pieces:
        result = result * levels(key, dims, pieces, -0.22, 0.18)
    return jnp.clip(with_spikes(result, jax.random.fold_in(key, 3), *heavy), -bound, bound).astype(kind)


def setup_inputs(seed: int = 0) -> dict:
    arg_keys = jax.random.split(jax.random.key(seed), 7)
    return {
        "features": scatter_about(arg_keys[0], (NODES, F), 1.0, 6.0, ((0, 32),)),
        "weight": scatter_about(arg_keys[1], (F, H), F ** -0.5, 0.25),
        "edge_tiles": noise_with(arg_keys[2], (CBLK, RBLK, RBLK, KR, BLK, BLK), (BLK * KR * RBLK // 2) ** -0.5, 0.3125, ((0, 8), (1, 4)), (1, 2, 4, 2.0)),
        "tile_col": draw_tile_col(jax.random.fold_in(arg_keys[6], 71), 0),
        "tile_count": draw_tile_count(jax.random.fold_in(arg_keys[6], 71), 0),
        "cotangent": scatter_about(arg_keys[5], (NODES, H), NODES ** -0.5, 0.09375, ((0, 32),)),
    }


def reference(features, weight, edge_tiles, tile_col, tile_count, cotangent):
    node_blocks = features.reshape(CBLK * RBLK, BLK, F)

    def row_group(row_index):
        def one_entry(col_index):
            column_ids = tile_col[row_index, col_index] * RBLK + col_index
            picked = node_blocks[column_ids].astype(jnp.float32)
            is_live = jnp.arange(KR, dtype=jnp.int32)[None, :] < tile_count[row_index, col_index][:, None]
            masked = edge_tiles[row_index, col_index].astype(jnp.float32) * is_live[:, :, None, None].astype(jnp.float32)
            return jnp.einsum('akij,akjf->aif', masked, picked).astype(jnp.bfloat16)

        entry_terms = lax.map(one_entry, jnp.arange(RBLK, dtype=jnp.int32))
        return jnp.sum(entry_terms.astype(jnp.float32), axis=0).astype(jnp.bfloat16)

    aggregated = lax.map(row_group, jnp.arange(CBLK, dtype=jnp.int32)).reshape(NODES, F)
    preact = jnp.dot(aggregated, weight, preferred_element_type=jnp.float32)
    sigmoid_pre = jax.nn.sigmoid(preact)
    activations = (preact * sigmoid_pre).astype(jnp.bfloat16)
    pre_grad = (cotangent.astype(jnp.float32) * sigmoid_pre * (1.0 + preact * (1.0 - sigmoid_pre))).astype(jnp.bfloat16)
    weight_grad = jnp.dot(aggregated.T, pre_grad, preferred_element_type=jnp.float32)
    return activations, weight_grad
```

```python
import jax
import jax.numpy as jnp
from jax import lax
from jax.sharding import PartitionSpec as P


def swap(value, axis, bits, size):
    return lax.ppermute(value, axis, [(i, i ^ bits) for i in range(size)])


def make_local(rows, cols):
    chips = rows // 2

    def local(features, weight, edge_tiles, tile_col, tile_count, cotangent):
        block, width = features.shape
        row_blocks, slots = edge_tiles.shape[2:4]
        my_row = lax.axis_index("row")
        my_col = lax.axis_index("col")
        core, chip = my_row % 2, my_row // 2

        even = [features] + [swap(features, "row", 2 * k, rows) for k in range(1, chips)]
        even = jnp.concatenate(even)
        odd = swap(even, "row", 1, rows)

        order = jnp.arange(row_blocks) ^ my_col
        tiles = edge_tiles[0, 0][order]
        counts = tile_count[0, 0][order]
        position = tile_col[0, 0][order] ^ my_row
        live = jnp.arange(slots)[None, :] < counts[:, None]
        position = jnp.where(live, position, rows)

        def dense(parity):
            places = 2 * jnp.arange(chips) + parity
            pick = position[:, :, None] == places[None, None, :]
            out = jnp.zeros((row_blocks, block, chips, block), jnp.bfloat16)
            for slot in range(slots):
                out = jnp.where(
                    pick[:, slot, None, :, None], tiles[:, slot, :, None, :], out
                )
            return out.reshape(row_blocks * block, chips * block)

        terms = jnp.dot(dense(0), even, preferred_element_type=jnp.float32)
        terms = terms + jnp.dot(dense(1), odd, preferred_element_type=jnp.float32)
        terms = terms.astype(jnp.bfloat16).reshape(row_blocks, block, width)

        got = [swap(terms[k], "col", k, cols) for k in range(1, cols)]
        total = terms[0].astype(jnp.float32)
        for part in got:
            total = total + part.astype(jnp.float32)
        aggregated = total.astype(jnp.bfloat16)

        preact = jnp.dot(aggregated, weight, preferred_element_type=jnp.float32)
        sigmoid_pre = jax.nn.sigmoid(preact)
        activations = (preact * sigmoid_pre).astype(jnp.bfloat16)
        pre_grad = (
            cotangent.astype(jnp.float32) * sigmoid_pre * (1.0 + preact * (1.0 - sigmoid_pre))
        ).astype(jnp.bfloat16)
        grad = lax.dot_general(
            aggregated, pre_grad, (((0,), (0,)), ((), ())), preferred_element_type=jnp.float32
        )

        hidden = weight.shape[1]
        half = width // 2
        piece = half // chips
        grad = grad.reshape(2, half, hidden)
        sent = lax.dynamic_index_in_dim(grad, 1 - core, 0, keepdims=False).astype(jnp.bfloat16)
        kept = lax.dynamic_index_in_dim(grad, core, 0, keepdims=False)
        kept = kept + swap(sent, "row", 1, rows).astype(jnp.float32)
        kept = kept.reshape(chips, piece, hidden)
        mine = lax.dynamic_index_in_dim(kept, chip, 0, keepdims=False)
        others = [
            lax.dynamic_index_in_dim(kept, chip ^ k, 0, keepdims=False).astype(jnp.bfloat16)
            for k in range(1, chips)
        ]
        for k in range(1, chips):
            mine = mine + swap(others[k - 1], "row", 2 * k, rows).astype(jnp.float32)
        mine = mine.astype(jnp.bfloat16)
        parts = [mine] + [swap(mine, "col", k, cols) for k in range(1, cols)]
        parts = [part.astype(jnp.float32) for part in parts]
        while len(parts) > 1:
            parts = [parts[i] + parts[i + 1] for i in range(0, len(parts), 2)]
        mine = parts[0].astype(jnp.bfloat16)
        kept = jnp.zeros((chips, piece, hidden), jnp.bfloat16)
        kept = lax.dynamic_update_index_in_dim(kept, mine, chip, 0)
        for k in range(1, chips):
            kept = lax.dynamic_update_index_in_dim(
                kept, swap(mine, "row", 2 * k, rows), chip ^ k, 0
            )
        kept = kept.reshape(half, hidden)
        other = swap(kept, "row", 1, rows)
        first = jnp.where(core == 0, kept, other)
        second = jnp.where(core == 0, other, kept)
        weight_grad = jnp.concatenate([first, second]).astype(jnp.float32)
        return (activations, weight_grad)

    return local


def solution(mesh):
    return jax.shard_map(
        make_local(mesh.shape["row"], mesh.shape["col"]),
        mesh=mesh,
        in_specs=(
            P(("row", "col"), None),
            P(),
            P("row", "col", None, None, None, None),
            P("row", "col", None, None),
            P("row", "col", None),
            P(("row", "col"), None),
        ),
        out_specs=(P(("row", "col"), None), P()),
        check_vma=False,
    )
```

```python
import jax
import jax.numpy as jnp
from jax import lax
from jax.sharding import PartitionSpec as P


def make_local(rows, cols):
    chips = rows // 2
    alike = chips == cols

    def over_row(value, bits):
        return lax.ppermute(value, "row", [(i, i ^ bits) for i in range(rows)])

    def over_col(value, bits):
        return lax.ppermute(value, "col", [(i, i ^ bits) for i in range(cols)])

    def by_core(value, bits, flip):
        pairs = []
        for i in range(rows):
            for j in range(cols):
                if i % 2 == flip:
                    target = (i ^ (2 * bits)) * cols + j
                else:
                    target = i * cols + (j ^ bits)
                pairs.append((i * cols + j, target))
        return lax.ppermute(value, ("row", "col"), pairs)

    def local(features, weight, edge_tiles, tile_col, tile_count, cotangent):
        block, width = features.shape
        row_blocks, slots = edge_tiles.shape[2:4]
        my_row = lax.axis_index("row")
        my_col = lax.axis_index("col")
        core, chip = my_row % 2, my_row // 2

        far = [over_row(features, 2 * k) for k in range(chips - 1, 0, -1)]
        even = jnp.concatenate([features] + far)
        odd = over_row(even, 1)

        order = jnp.arange(row_blocks) ^ my_col
        tiles = edge_tiles[0, 0][order]
        counts = tile_count[0, 0][order]
        position = tile_col[0, 0][order] ^ my_row
        live = jnp.arange(slots)[None, :] < counts[:, None]
        position = jnp.where(live, position, rows)

        def dense(parity):
            places = 2 * (-jnp.arange(chips) % chips) + parity
            pick = position[:, :, None] == places[None, None, :]
            out = jnp.zeros((row_blocks, block, chips, block), jnp.bfloat16)
            for slot in range(slots):
                out = jnp.where(
                    pick[:, slot, None, :, None], tiles[:, slot, :, None, :], out
                )
            return out.reshape(row_blocks, block, chips * block)

        near_part = jnp.dot(
            dense(0).reshape(row_blocks * block, chips * block),
            even,
            preferred_element_type=jnp.float32,
        ).reshape(row_blocks, block, width)
        adjacency = dense(1)

        def term(k):
            part = jnp.dot(adjacency[k], odd, preferred_element_type=jnp.float32)
            return (near_part[k] + part).astype(jnp.bfloat16)

        got = [over_col(term(k), k) for k in range(cols - 1, 0, -1)]
        total = term(0).astype(jnp.float32)
        for part in got:
            total = total + part.astype(jnp.float32)
        aggregated = total.astype(jnp.bfloat16)

        preact = jnp.dot(aggregated, weight, preferred_element_type=jnp.float32)
        sigmoid_pre = jax.nn.sigmoid(preact)
        activations = (preact * sigmoid_pre).astype(jnp.bfloat16)
        pre_grad = (
            cotangent.astype(jnp.float32) * sigmoid_pre * (1.0 + preact * (1.0 - sigmoid_pre))
        ).astype(jnp.bfloat16)
        grad = lax.dot_general(
            aggregated, pre_grad, (((0,), (0,)), ((), ())), preferred_element_type=jnp.float32
        )

        hidden = weight.shape[1]
        half = width // 2
        grad = grad.reshape(2, half, hidden)
        sent = lax.dynamic_index_in_dim(grad, 1 - core, 0, keepdims=False).astype(jnp.bfloat16)
        kept = lax.dynamic_index_in_dim(grad, core, 0, keepdims=False)
        kept = kept + over_row(sent, 1).astype(jnp.float32)
        if alike:
            place = jnp.where(core == 0, chip, my_col)
            shares, first = chips, lambda value, k: by_core(value, k, 0)
            peers, second = cols, lambda value, k: by_core(value, k, 1)
        else:
            place = chip
            shares, first = chips, lambda value, k: over_row(value, 2 * k)
            peers, second = cols, over_col
        piece = half // shares
        kept = kept.reshape(shares, piece, hidden)
        mine = lax.dynamic_index_in_dim(kept, place, 0, keepdims=False)
        for k in range(1, shares):
            other = lax.dynamic_index_in_dim(kept, place ^ k, 0, keepdims=False)
            mine = mine + first(other.astype(jnp.bfloat16), k).astype(jnp.float32)
        mine = mine.astype(jnp.bfloat16)
        parts = [second(mine, k) for k in range(peers - 1, 0, -1)] + [mine]
        parts = [part.astype(jnp.float32) for part in parts]
        while len(parts) > 1:
            parts = [parts[i] + parts[i + 1] for i in range(0, len(parts), 2)]
        mine = parts[0].astype(jnp.bfloat16)
        kept = jnp.zeros((shares, piece, hidden), jnp.bfloat16)
        for k in range(shares - 1, 0, -1):
            kept = lax.dynamic_update_index_in_dim(kept, first(mine, k), place ^ k, 0)
        kept = lax.dynamic_update_index_in_dim(kept, mine, place, 0)
        kept = kept.reshape(half, hidden)
        other = over_row(kept, 1)
        weight_grad = jnp.zeros((2, half, hidden), jnp.float32)
        weight_grad = lax.dynamic_update_index_in_dim(
            weight_grad, kept.astype(jnp.float32), core, 0
        )
        weight_grad = lax.dynamic_update_index_in_dim(
            weight_grad, other.astype(jnp.float32), 1 - core, 0
        )
        return (activations, weight_grad.reshape(width, hidden))

    return local


def solution(mesh):
    return jax.shard_map(
        make_local(mesh.shape["row"], mesh.shape["col"]),
        mesh=mesh,
        in_specs=(
            P(("row", "col"), None),
            P(),
            P("row", "col", None, None, None, None),
            P("row", "col", None, None),
            P("row", "col", None),
            P(("row", "col"), None),
        ),
        out_specs=(P(("row", "col"), None), P()),
        check_vma=False,
    )
```

```python
import functools

import jax
import jax.numpy as jnp
from jax import lax
from jax.experimental import pallas as pl
from jax.experimental.pallas import tpu as pltpu
from jax.sharding import PartitionSpec as P

LIMIT = 8 * 1024 * 1024
VMEM = pl.BlockSpec(memory_space=pltpu.VMEM)
SMEM = pl.BlockSpec(memory_space=pltpu.SMEM)
HBM = pl.BlockSpec(memory_space=pltpu.HBM)


def columns_of(ref, half, size):
    return ref[:, pl.ds(pl.multiple_of(half * size, size), size)]


def grad_half(agg_ref, pre_grad, half, size):
    return lax.dot_general(
        columns_of(agg_ref, half, size),
        pre_grad,
        (((0,), (0,)), ((), ())),
        preferred_element_type=jnp.float32,
    )


def dense_kernel(half_ref, *refs):
    parts, (weight_ref, cot_ref), (agg_ref, preact_ref, pre_ref, sent_ref) = (
        refs[:-6],
        refs[-6:-4],
        refs[-4:],
    )
    total = parts[0][...].astype(jnp.float32)
    for part in parts[1:]:
        total = total + part[...].astype(jnp.float32)
    agg_ref[...] = total.astype(jnp.bfloat16)
    preact = jnp.dot(agg_ref[...], weight_ref[...], preferred_element_type=jnp.float32)
    sigmoid = jax.nn.sigmoid(preact)
    preact_ref[...] = preact
    pre_ref[...] = (
        cot_ref[...].astype(jnp.float32) * sigmoid * (1.0 + preact * (1.0 - sigmoid))
    ).astype(jnp.bfloat16)
    size = sent_ref.shape[0]
    sent_ref[...] = grad_half(agg_ref, pre_ref[...], 1 - half_ref[0], size).astype(jnp.bfloat16)


def kept_kernel(half_ref, agg_ref, pre_ref, preact_ref, kept_ref, act_ref):
    preact = preact_ref[...]
    act_ref[...] = (preact * jax.nn.sigmoid(preact)).astype(jnp.bfloat16)
    kept_ref[...] = grad_half(agg_ref, pre_ref[...], half_ref[0], kept_ref.shape[0])


def first_kernel(half_ref, kept_ref, out_ref, wide_ref, sem):
    wide_ref[...] = kept_ref[...].astype(jnp.float32)
    copy = pltpu.make_async_copy(wide_ref, out_ref.at[half_ref[0]], sem)
    copy.start()
    copy.wait()


def second_kernel(half_ref, other_ref, _, out_ref, wide_ref, sems):
    pieces, size, _ = wide_ref.shape
    copies = []
    for i in range(pieces):
        rows = pl.ds(i * size, size)
        wide_ref[i] = other_ref[rows, :].astype(jnp.float32)
        copies.append(
            pltpu.make_async_copy(wide_ref.at[i], out_ref.at[1 - half_ref[0], rows], sems.at[i])
        )
        copies[-1].start()
    for copy in copies:
        copy.wait()


def write_first(half, kept):
    size, hidden = kept.shape
    return pl.pallas_call(
        first_kernel,
        out_shape=jax.ShapeDtypeStruct((2, size, hidden), jnp.float32),
        in_specs=[SMEM, VMEM],
        out_specs=HBM,
        scratch_shapes=[pltpu.VMEM((size, hidden), jnp.float32), pltpu.SemaphoreType.DMA],
        compiler_params=pltpu.CompilerParams(vmem_limit_bytes=LIMIT),
        cost_estimate=pl.CostEstimate(
            flops=size * hidden, bytes_accessed=6 * size * hidden, transcendentals=0
        ),
    )(half, kept)


def write_second(half, other, out):
    size, hidden = other.shape
    pieces = 4
    return pl.pallas_call(
        second_kernel,
        out_shape=jax.ShapeDtypeStruct(out.shape, out.dtype),
        in_specs=[SMEM, VMEM, HBM],
        out_specs=HBM,
        scratch_shapes=[
            pltpu.VMEM((pieces, size // pieces, hidden), jnp.float32),
            pltpu.SemaphoreType.DMA((pieces,)),
        ],
        input_output_aliases={2: 0},
        compiler_params=pltpu.CompilerParams(vmem_limit_bytes=LIMIT),
        cost_estimate=pl.CostEstimate(
            flops=size * hidden, bytes_accessed=6 * size * hidden, transcendentals=0
        ),
    )(half, other, out)


def dense_part(half, parts, weight, cotangent):
    block, width = parts[0].shape
    hidden = weight.shape[1]
    size = width // 2
    agg, preact, pre, sent = pl.pallas_call(
        dense_kernel,
        out_shape=(
            jax.ShapeDtypeStruct((block, width), jnp.bfloat16),
            jax.ShapeDtypeStruct((block, hidden), jnp.float32),
            jax.ShapeDtypeStruct((block, hidden), jnp.bfloat16),
            jax.ShapeDtypeStruct((size, hidden), jnp.bfloat16),
        ),
        in_specs=[SMEM] + [VMEM] * (len(parts) + 2),
        out_specs=(VMEM,) * 4,
        compiler_params=pltpu.CompilerParams(vmem_limit_bytes=LIMIT),
        cost_estimate=pl.CostEstimate(
            flops=3 * block * width * hidden, bytes_accessed=8 * block * width, transcendentals=0
        ),
    )(half, *parts, weight, cotangent)
    kept, act = pl.pallas_call(
        kept_kernel,
        out_shape=(
            jax.ShapeDtypeStruct((size, hidden), jnp.float32),
            jax.ShapeDtypeStruct((block, hidden), jnp.bfloat16),
        ),
        in_specs=[SMEM] + [VMEM] * 3,
        out_specs=(VMEM,) * 2,
        compiler_params=pltpu.CompilerParams(vmem_limit_bytes=LIMIT),
        cost_estimate=pl.CostEstimate(
            flops=block * width * hidden, bytes_accessed=4 * block * width, transcendentals=0
        ),
    )(half, agg, pre, preact)
    return act, sent, kept


def make_local(rows, cols):
    chips = rows // 2

    def over_row(value, bits):
        return lax.ppermute(value, "row", [(i, i ^ bits) for i in range(rows)])

    def over_col(value, bits):
        return lax.ppermute(value, "col", [(i, i ^ bits) for i in range(cols)])

    masks = [2 * k + bin(k).count("1") % 2 for k in range(chips)]

    def local(features, weight, edge_tiles, tile_col, tile_count, cotangent):
        block, width = features.shape
        row_blocks, slots = edge_tiles.shape[2:4]
        my_row = lax.axis_index("row")
        my_col = lax.axis_index("col")
        chip = my_row // 2

        far = [over_row(features, 2 * k) for k in range(chips - 1, 0, -1)]
        even = jnp.concatenate([features] + far)
        odd = over_row(even, 1)

        order = jnp.arange(row_blocks) ^ my_col
        tiles = edge_tiles[0, 0][order]
        counts = tile_count[0, 0][order]
        position = tile_col[0, 0][order] ^ my_row
        live = jnp.arange(slots)[None, :] < counts[:, None]
        position = jnp.where(live, position, rows)

        def dense(parity):
            places = 2 * (-jnp.arange(chips) % chips) + parity
            pick = position[:, :, None] == places[None, None, :]
            out = jnp.zeros((row_blocks, block, chips, block), jnp.bfloat16)
            for slot in range(slots):
                out = jnp.where(
                    pick[:, slot, None, :, None], tiles[:, slot, :, None, :], out
                )
            return out.reshape(row_blocks, block, chips * block)

        near_part = jnp.dot(
            dense(0).reshape(row_blocks * block, chips * block),
            even,
            preferred_element_type=jnp.float32,
        ).reshape(row_blocks, block, width)
        adjacency = dense(1)

        def term(k):
            part = jnp.dot(adjacency[k], odd, preferred_element_type=jnp.float32)
            return (near_part[k] + part).astype(jnp.bfloat16)

        turns = sorted(range(1, cols), key=lambda k: (k != cols - 1, k))
        got = [over_col(term(k), k) for k in turns]

        half = (my_row + sum((chip >> i) for i in range(chips.bit_length()))) % 2
        half = half.astype(jnp.int32)
        activations, sent, kept = dense_part(half[None], [term(0)] + got, weight, cotangent)

        size, hidden = sent.shape
        kept = kept + over_row(sent, 1).astype(jnp.float32)
        piece = size // chips
        kept = kept.reshape(chips, piece, hidden)
        mine = lax.dynamic_index_in_dim(kept, chip, 0, keepdims=False)
        for k in range(1, chips):
            other = lax.dynamic_index_in_dim(kept, chip ^ k, 0, keepdims=False)
            mine = mine + over_row(other.astype(jnp.bfloat16), masks[k]).astype(jnp.float32)
        mine = mine.astype(jnp.bfloat16)
        parts = [over_col(mine, k) for k in range(cols - 1, 0, -1)] + [mine]
        parts = [part.astype(jnp.float32) for part in parts]
        while len(parts) > 1:
            parts = [parts[i] + parts[i + 1] for i in range(0, len(parts), 2)]
        mine = parts[0].astype(jnp.bfloat16)
        kept = jnp.zeros((chips, piece, hidden), jnp.bfloat16)
        for k in range(chips - 1, 0, -1):
            kept = lax.dynamic_update_index_in_dim(kept, over_row(mine, masks[k]), chip ^ k, 0)
        kept = lax.dynamic_update_index_in_dim(kept, mine, chip, 0)
        kept = kept.reshape(size, hidden)
        other = over_row(kept, 1)
        weight_grad = write_first(half[None], kept)
        weight_grad = write_second(half[None], other, weight_grad)
        return (activations, weight_grad.reshape(width, hidden))

    return local


def solution(mesh):
    return jax.shard_map(
        make_local(mesh.shape["row"], mesh.shape["col"]),
        mesh=mesh,
        in_specs=(
            P(("row", "col"), None),
            P(),
            P("row", "col", None, None, None, None),
            P("row", "col", None, None),
            P("row", "col", None),
            P(("row", "col"), None),
        ),
        out_specs=(P(("row", "col"), None), P()),
        check_vma=False,
    )
```

```python
import functools

import jax
import jax.numpy as jnp
from jax import lax
from jax.experimental import pallas as pl
from jax.experimental.pallas import tpu as pltpu
from jax.sharding import PartitionSpec as P

LIMIT = 8 * 1024 * 1024
VMEM = pl.BlockSpec(memory_space=pltpu.VMEM)
SMEM = pl.BlockSpec(memory_space=pltpu.SMEM)
HBM = pl.BlockSpec(memory_space=pltpu.HBM)


def place_kernel(groups, ids_ref, col_ref, count_ref, tiles_ref, *out_refs):
    row_blocks, slots, block = tiles_ref.shape[2:5]
    rows = groups[-1][1] * 2
    chips = rows // 2
    for out_ref in out_refs:
        out_ref[...] = jnp.zeros_like(out_ref)
    for q in range(row_blocks):
        a = q ^ ids_ref[1]
        for k in range(slots):
            position = (col_ref[0, 0, a, k] ^ ids_ref[0]) & (rows - 1)
            slot = (chips - position // 2) % chips
            live = k < count_ref[0, 0, a]
            for (parity, last, first), out_ref in zip(groups, out_refs):
                here = (position % 2 == parity) & (slot >= first) & (slot < last)

                @pl.when(live & here)
                def _(out_ref=out_ref, first=first, q=q, k=k, a=a, slot=slot):
                    start = pl.multiple_of((slot - first) * block, block)
                    out_ref[pl.ds(q * block, block), pl.ds(start, block)] = tiles_ref[0, 0, a, k]


def placed(ids, tile_col, tile_count, edge_tiles, chips):
    row_blocks, _, block = edge_tiles.shape[2:5]
    early = chips // 2
    groups = ((0, early, 0), (1, early, 0), (0, chips, early), (1, chips, early))
    held = 4 * edge_tiles.size + 8 * row_blocks * chips * block * block
    return pl.pallas_call(
        functools.partial(place_kernel, groups),
        out_shape=tuple(
            jax.ShapeDtypeStruct((row_blocks * block, (last - first) * block), jnp.bfloat16)
            for _, last, first in groups
        ),
        in_specs=[SMEM] * 3 + [VMEM],
        out_specs=(VMEM,) * 4,
        compiler_params=pltpu.CompilerParams(vmem_limit_bytes=max(LIMIT, held)),
        cost_estimate=pl.CostEstimate(
            flops=edge_tiles.size, bytes_accessed=6 * edge_tiles.size, transcendentals=0
        ),
    )(ids, tile_col, tile_count, edge_tiles)


def columns_of(ref, half, size):
    return ref[:, pl.ds(pl.multiple_of(half * size, size), size)]


def grad_half(agg_ref, pre_grad, half, size):
    return lax.dot_general(
        columns_of(agg_ref, half, size),
        pre_grad,
        (((0,), (0,)), ((), ())),
        preferred_element_type=jnp.float32,
    )


def dense_kernel(half_ref, *refs):
    parts, (weight_ref, cot_ref), (agg_ref, preact_ref, pre_ref, sent_ref) = (
        refs[:-6],
        refs[-6:-4],
        refs[-4:],
    )
    total = parts[0][...].astype(jnp.float32)
    for part in parts[1:]:
        total = total + part[...].astype(jnp.float32)
    agg_ref[...] = total.astype(jnp.bfloat16)
    preact = jnp.dot(agg_ref[...], weight_ref[...], preferred_element_type=jnp.float32)
    sigmoid = jax.nn.sigmoid(preact)
    preact_ref[...] = preact
    pre_ref[...] = (
        cot_ref[...].astype(jnp.float32) * sigmoid * (1.0 + preact * (1.0 - sigmoid))
    ).astype(jnp.bfloat16)
    size = sent_ref.shape[0]
    sent_ref[...] = grad_half(agg_ref, pre_ref[...], 1 - half_ref[0], size).astype(jnp.bfloat16)


def kept_kernel(half_ref, agg_ref, pre_ref, preact_ref, kept_ref, act_ref):
    preact = preact_ref[...]
    act_ref[...] = (preact * jax.nn.sigmoid(preact)).astype(jnp.bfloat16)
    kept_ref[...] = grad_half(agg_ref, pre_ref[...], half_ref[0], kept_ref.shape[0])


def first_kernel(half_ref, kept_ref, out_ref, wide_ref, sem):
    wide_ref[...] = kept_ref[...].astype(jnp.float32)
    copy = pltpu.make_async_copy(wide_ref, out_ref.at[half_ref[0]], sem)
    copy.start()
    copy.wait()


def second_kernel(half_ref, other_ref, _, out_ref, wide_ref, sems):
    pieces, size, _ = wide_ref.shape
    copies = []
    for i in range(pieces):
        rows = pl.ds(i * size, size)
        wide_ref[i] = other_ref[rows, :].astype(jnp.float32)
        copies.append(
            pltpu.make_async_copy(wide_ref.at[i], out_ref.at[1 - half_ref[0], rows], sems.at[i])
        )
        copies[-1].start()
    for copy in copies:
        copy.wait()


def write_first(half, kept):
    size, hidden = kept.shape
    return pl.pallas_call(
        first_kernel,
        out_shape=jax.ShapeDtypeStruct((2, size, hidden), jnp.float32),
        in_specs=[SMEM, VMEM],
        out_specs=HBM,
        scratch_shapes=[pltpu.VMEM((size, hidden), jnp.float32), pltpu.SemaphoreType.DMA],
        compiler_params=pltpu.CompilerParams(vmem_limit_bytes=LIMIT),
        cost_estimate=pl.CostEstimate(
            flops=size * hidden, bytes_accessed=6 * size * hidden, transcendentals=0
        ),
    )(half, kept)


def write_second(half, other, out):
    size, hidden = other.shape
    pieces = 4
    return pl.pallas_call(
        second_kernel,
        out_shape=jax.ShapeDtypeStruct(out.shape, out.dtype),
        in_specs=[SMEM, VMEM, HBM],
        out_specs=HBM,
        scratch_shapes=[
            pltpu.VMEM((pieces, size // pieces, hidden), jnp.float32),
            pltpu.SemaphoreType.DMA((pieces,)),
        ],
        input_output_aliases={2: 0},
        compiler_params=pltpu.CompilerParams(vmem_limit_bytes=LIMIT),
        cost_estimate=pl.CostEstimate(
            flops=size * hidden, bytes_accessed=6 * size * hidden, transcendentals=0
        ),
    )(half, other, out)


def dense_part(half, parts, weight, cotangent):
    block, width = parts[0].shape
    hidden = weight.shape[1]
    size = width // 2
    agg, preact, pre, sent = pl.pallas_call(
        dense_kernel,
        out_shape=(
            jax.ShapeDtypeStruct((block, width), jnp.bfloat16),
            jax.ShapeDtypeStruct((block, hidden), jnp.float32),
            jax.ShapeDtypeStruct((block, hidden), jnp.bfloat16),
            jax.ShapeDtypeStruct((size, hidden), jnp.bfloat16),
        ),
        in_specs=[SMEM] + [VMEM] * (len(parts) + 2),
        out_specs=(VMEM,) * 4,
        compiler_params=pltpu.CompilerParams(vmem_limit_bytes=LIMIT),
        cost_estimate=pl.CostEstimate(
            flops=3 * block * width * hidden, bytes_accessed=8 * block * width, transcendentals=0
        ),
    )(half, *parts, weight, cotangent)
    kept, act = pl.pallas_call(
        kept_kernel,
        out_shape=(
            jax.ShapeDtypeStruct((size, hidden), jnp.float32),
            jax.ShapeDtypeStruct((block, hidden), jnp.bfloat16),
        ),
        in_specs=[SMEM] + [VMEM] * 3,
        out_specs=(VMEM,) * 2,
        compiler_params=pltpu.CompilerParams(vmem_limit_bytes=LIMIT),
        cost_estimate=pl.CostEstimate(
            flops=block * width * hidden, bytes_accessed=4 * block * width, transcendentals=0
        ),
    )(half, agg, pre, preact)
    return act, sent, kept


def make_local(rows, cols):
    chips = rows // 2

    def over_row(value, bits):
        return lax.ppermute(value, "row", [(i, i ^ bits) for i in range(rows)])

    def over_col(value, bits):
        return lax.ppermute(value, "col", [(i, i ^ bits) for i in range(cols)])

    def by_core(value, bits, flip):
        pairs = []
        for i in range(rows):
            for j in range(cols):
                if i % 2 == flip:
                    target = (i ^ (2 * bits)) * cols + j
                else:
                    target = i * cols + (j ^ bits)
                pairs.append((i * cols + j, target))
        return lax.ppermute(value, ("row", "col"), pairs)

    def local(features, weight, edge_tiles, tile_col, tile_count, cotangent):
        block, width = features.shape
        my_row = lax.axis_index("row")
        my_col = lax.axis_index("col")
        chip = my_row // 2

        far = [over_row(features, 2 * k) for k in range(chips - 1, 0, -1)]
        early = chips // 2
        even_a = jnp.concatenate([features] + far[: early - 1])
        odd_a = over_row(even_a, 1)
        even_b = jnp.concatenate(far[early - 1 :])
        odd_b = over_row(even_b, 1)

        ids = jnp.stack([my_row, my_col]).astype(jnp.int32)
        left = placed(ids, tile_col, tile_count, edge_tiles, chips)

        def product(one, other):
            return jnp.dot(one, other, preferred_element_type=jnp.float32)

        near_part = product(left[0], even_a) + product(left[1], odd_a) + product(left[2], even_b)

        def term(k):
            at = slice(k * block, (k + 1) * block)
            return (near_part[at] + product(left[3][at], odd_b)).astype(jnp.bfloat16)

        turns = sorted(range(1, cols), key=lambda k: (k != cols - 1, k))
        got = [over_col(term(k), k) for k in turns]

        half = (my_row % 2).astype(jnp.int32)
        activations, sent, kept = dense_part(half[None], [term(0)] + got, weight, cotangent)

        size, hidden = sent.shape
        kept = kept + over_row(sent, 1).astype(jnp.float32)
        if chips == cols:
            place = jnp.where(my_row % 2 == 0, chip, my_col)
            first = lambda value, k: by_core(value, k, 0)
            second = lambda value, k: by_core(value, k, 1)
        else:
            place = chip
            first = lambda value, k: over_row(value, 2 * k)
            second = over_col
        piece = size // chips
        kept = kept.reshape(chips, piece, hidden)
        mine = lax.dynamic_index_in_dim(kept, place, 0, keepdims=False)
        for k in range(1, chips):
            other = lax.dynamic_index_in_dim(kept, place ^ k, 0, keepdims=False)
            mine = mine + first(other.astype(jnp.bfloat16), k).astype(jnp.float32)
        mine = mine.astype(jnp.bfloat16)
        parts = [second(mine, k) for k in range(cols - 1, 0, -1)] + [mine]
        parts = [part.astype(jnp.float32) for part in parts]
        while len(parts) > 1:
            parts = [parts[i] + parts[i + 1] for i in range(0, len(parts), 2)]
        mine = parts[0].astype(jnp.bfloat16)
        kept = jnp.zeros((chips, piece, hidden), jnp.bfloat16)
        for k in range(chips - 1, 0, -1):
            kept = lax.dynamic_update_index_in_dim(kept, first(mine, k), place ^ k, 0)
        kept = lax.dynamic_update_index_in_dim(kept, mine, place, 0)
        kept = kept.reshape(size, hidden)
        other = over_row(kept, 1)
        weight_grad = write_first(half[None], kept)
        weight_grad = write_second(half[None], other, weight_grad)
        return (activations, weight_grad.reshape(width, hidden))

    return local


def solution(mesh):
    return jax.shard_map(
        make_local(mesh.shape["row"], mesh.shape["col"]),
        mesh=mesh,
        in_specs=(
            P(("row", "col"), None),
            P(),
            P("row", "col", None, None, None, None),
            P("row", "col", None, None),
            P("row", "col", None),
            P(("row", "col"), None),
        ),
        out_specs=(P(("row", "col"), None), P()),
        check_vma=False,
    )
```

```python
import functools

import jax
import jax.numpy as jnp
from jax import lax
from jax.experimental import pallas as pl
from jax.experimental.pallas import tpu as pltpu
from jax.sharding import PartitionSpec as P

LIMIT = 8 * 1024 * 1024
VMEM = pl.BlockSpec(memory_space=pltpu.VMEM)
SMEM = pl.BlockSpec(memory_space=pltpu.SMEM)
HBM = pl.BlockSpec(memory_space=pltpu.HBM)


def place_kernel(groups, ids_ref, col_ref, count_ref, tiles_ref, *out_refs):
    row_blocks, slots, block = tiles_ref.shape[2:5]
    rows = groups[-1][1] * 2
    chips = rows // 2
    for out_ref in out_refs:
        out_ref[...] = jnp.zeros_like(out_ref)
    for q in range(row_blocks):
        a = q ^ ids_ref[1]
        for k in range(slots):
            position = (col_ref[0, 0, a, k] ^ ids_ref[0]) & (rows - 1)
            slot = (chips - position // 2) % chips
            live = k < count_ref[0, 0, a]
            for (parity, last, first), out_ref in zip(groups, out_refs):
                here = (position % 2 == parity) & (slot >= first) & (slot < last)

                @pl.when(live & here)
                def _(out_ref=out_ref, first=first, q=q, k=k, a=a, slot=slot):
                    start = pl.multiple_of((slot - first) * block, block)
                    out_ref[pl.ds(q * block, block), pl.ds(start, block)] = tiles_ref[0, 0, a, k]


def placed(ids, tile_col, tile_count, edge_tiles, chips):
    row_blocks, _, block = edge_tiles.shape[2:5]
    early = chips // 2
    groups = ((0, early, 0), (1, early, 0), (0, chips, early), (1, chips, early))
    held = 4 * edge_tiles.size + 8 * row_blocks * chips * block * block
    return pl.pallas_call(
        functools.partial(place_kernel, groups),
        out_shape=tuple(
            jax.ShapeDtypeStruct((row_blocks * block, (last - first) * block), jnp.bfloat16)
            for _, last, first in groups
        ),
        in_specs=[SMEM] * 3 + [VMEM],
        out_specs=(VMEM,) * 4,
        compiler_params=pltpu.CompilerParams(vmem_limit_bytes=max(LIMIT, held)),
        cost_estimate=pl.CostEstimate(
            flops=edge_tiles.size, bytes_accessed=6 * edge_tiles.size, transcendentals=0
        ),
    )(ids, tile_col, tile_count, edge_tiles)


def columns_of(ref, half, size):
    return ref[:, pl.ds(pl.multiple_of(half * size, size), size)]


def grad_half(agg_ref, pre_grad, half, size):
    return lax.dot_general(
        columns_of(agg_ref, half, size),
        pre_grad,
        (((0,), (0,)), ((), ())),
        preferred_element_type=jnp.float32,
    )


def dense_kernel(half_ref, *refs):
    parts, (weight_ref, cot_ref), (agg_ref, preact_ref, pre_ref, sent_ref) = (
        refs[:-6],
        refs[-6:-4],
        refs[-4:],
    )
    total = parts[0][...].astype(jnp.float32)
    for part in parts[1:]:
        total = total + part[...].astype(jnp.float32)
    agg_ref[...] = total.astype(jnp.bfloat16)
    preact = jnp.dot(agg_ref[...], weight_ref[...], preferred_element_type=jnp.float32)
    sigmoid = jax.nn.sigmoid(preact)
    preact_ref[...] = preact
    pre_ref[...] = (
        cot_ref[...].astype(jnp.float32) * sigmoid * (1.0 + preact * (1.0 - sigmoid))
    ).astype(jnp.bfloat16)
    size = sent_ref.shape[0]
    sent_ref[...] = grad_half(agg_ref, pre_ref[...], 1 - half_ref[0], size).astype(jnp.bfloat16)


def kept_kernel(half_ref, agg_ref, pre_ref, preact_ref, kept_ref, act_ref):
    preact = preact_ref[...]
    act_ref[...] = (preact * jax.nn.sigmoid(preact)).astype(jnp.bfloat16)
    kept_ref[...] = grad_half(agg_ref, pre_ref[...], half_ref[0], kept_ref.shape[0])


def write_kernel(turns, half_ref, own_ref, other_ref, *refs):
    sources, (out_ref, wide_ref, sems) = refs[: len(turns)], refs[-3:]
    size = wide_ref.shape[1]
    copies = []
    for (flip, partners), source in zip(turns, sources):
        half = 1 - half_ref[0] if flip else half_ref[0]
        place = other_ref[0] if flip else own_ref[0]
        for i, k in enumerate(partners):
            n = len(copies)
            wide_ref[n] = source[pl.ds(i * size, size), :].astype(jnp.float32)
            target = out_ref.at[half, place ^ k]
            copies.append(pltpu.make_async_copy(wide_ref.at[n], target, sems.at[n]))
            copies[-1].start()
    for copy in copies:
        copy.wait()


def write(where, turns, sources, shape, out=None):
    size, hidden = shape[2:]
    total = sum(len(partners) for _, partners in turns)
    earlier = [] if out is None else [out]
    return pl.pallas_call(
        functools.partial(write_kernel, turns),
        out_shape=jax.ShapeDtypeStruct(shape, jnp.float32),
        in_specs=[SMEM] * 3 + [VMEM] * len(sources) + [HBM] * len(earlier),
        out_specs=HBM,
        scratch_shapes=[
            pltpu.VMEM((total, size, hidden), jnp.float32),
            pltpu.SemaphoreType.DMA((total,)),
        ],
        input_output_aliases={3 + len(sources): 0} if earlier else {},
        compiler_params=pltpu.CompilerParams(vmem_limit_bytes=LIMIT),
        cost_estimate=pl.CostEstimate(
            flops=total * size * hidden, bytes_accessed=6 * total * size * hidden, transcendentals=0
        ),
    )(*where, *sources, *earlier)


def dense_part(half, parts, weight, cotangent):
    block, width = parts[0].shape
    hidden = weight.shape[1]
    size = width // 2
    agg, preact, pre, sent = pl.pallas_call(
        dense_kernel,
        out_shape=(
            jax.ShapeDtypeStruct((block, width), jnp.bfloat16),
            jax.ShapeDtypeStruct((block, hidden), jnp.float32),
            jax.ShapeDtypeStruct((block, hidden), jnp.bfloat16),
            jax.ShapeDtypeStruct((size, hidden), jnp.bfloat16),
        ),
        in_specs=[SMEM] + [VMEM] * (len(parts) + 2),
        out_specs=(VMEM,) * 4,
        compiler_params=pltpu.CompilerParams(vmem_limit_bytes=LIMIT),
        cost_estimate=pl.CostEstimate(
            flops=3 * block * width * hidden, bytes_accessed=8 * block * width, transcendentals=0
        ),
    )(half, *parts, weight, cotangent)
    kept, act = pl.pallas_call(
        kept_kernel,
        out_shape=(
            jax.ShapeDtypeStruct((size, hidden), jnp.float32),
            jax.ShapeDtypeStruct((block, hidden), jnp.bfloat16),
        ),
        in_specs=[SMEM] + [VMEM] * 3,
        out_specs=(VMEM,) * 2,
        compiler_params=pltpu.CompilerParams(vmem_limit_bytes=LIMIT),
        cost_estimate=pl.CostEstimate(
            flops=block * width * hidden, bytes_accessed=4 * block * width, transcendentals=0
        ),
    )(half, agg, pre, preact)
    return act, sent, kept


def make_local(rows, cols):
    chips = rows // 2

    def over_row(value, bits):
        return lax.ppermute(value, "row", [(i, i ^ bits) for i in range(rows)])

    def over_col(value, bits):
        return lax.ppermute(value, "col", [(i, i ^ bits) for i in range(cols)])

    def by_core(value, bits, flip):
        pairs = []
        for i in range(rows):
            for j in range(cols):
                if i % 2 == flip:
                    target = (i ^ (2 * bits)) * cols + j
                else:
                    target = i * cols + (j ^ bits)
                pairs.append((i * cols + j, target))
        return lax.ppermute(value, ("row", "col"), pairs)

    def local(features, weight, edge_tiles, tile_col, tile_count, cotangent):
        block, width = features.shape
        my_row = lax.axis_index("row")
        my_col = lax.axis_index("col")
        chip = my_row // 2

        far = [over_row(features, 2 * k) for k in range(chips - 1, 0, -1)]
        early = chips // 2
        even_a = jnp.concatenate([features] + far[: early - 1])
        odd_a = over_row(even_a, 1)
        even_b = jnp.concatenate(far[early - 1 :])
        odd_b = over_row(even_b, 1)

        ids = jnp.stack([my_row, my_col]).astype(jnp.int32)
        left = placed(ids, tile_col, tile_count, edge_tiles, chips)

        def product(one, other):
            return jnp.dot(one, other, preferred_element_type=jnp.float32)

        near_part = product(left[0], even_a) + product(left[1], odd_a) + product(left[2], even_b)

        def term(k):
            at = slice(k * block, (k + 1) * block)
            return (near_part[at] + product(left[3][at], odd_b)).astype(jnp.bfloat16)

        turns = sorted(range(1, cols), key=lambda k: (k != cols - 1, k))
        got = [over_col(term(k), k) for k in turns]

        half = (my_row % 2).astype(jnp.int32)
        activations, sent, kept = dense_part(half[None], [term(0)] + got, weight, cotangent)

        size, hidden = sent.shape
        kept = kept + over_row(sent, 1).astype(jnp.float32)
        if chips == cols:
            place = jnp.where(my_row % 2 == 0, chip, my_col)
            place_other = jnp.where(my_row % 2 == 0, my_col, chip)
            first = lambda value, k: by_core(value, k, 0)
            second = lambda value, k: by_core(value, k, 1)
        else:
            place = place_other = chip
            first = lambda value, k: over_row(value, 2 * k)
            second = over_col
        piece = size // chips
        kept = kept.reshape(chips, piece, hidden)
        mine = lax.dynamic_index_in_dim(kept, place, 0, keepdims=False)
        for k in range(1, chips):
            other = lax.dynamic_index_in_dim(kept, place ^ k, 0, keepdims=False)
            mine = mine + first(other.astype(jnp.bfloat16), k).astype(jnp.float32)
        mine = mine.astype(jnp.bfloat16)
        parts = [second(mine, k) for k in range(cols - 1, 0, -1)] + [mine]
        parts = [part.astype(jnp.float32) for part in parts]
        while len(parts) > 1:
            parts = [parts[i] + parts[i + 1] for i in range(0, len(parts), 2)]
        mine = parts[0].astype(jnp.bfloat16)
        gathered = [first(mine, k) for k in range(chips - 1, 0, -1)]
        soon = [0] + list(range(chips - 1, early, -1))
        late = list(range(early, 0, -1))
        kept_a = jnp.concatenate([mine] + gathered[: early - 1])
        other_a = over_row(kept_a, 1)
        kept_b = jnp.concatenate(gathered[early - 1 :])
        other_b = over_row(kept_b, 1)
        where = [value.astype(jnp.int32)[None] for value in (half, place, place_other)]
        shape = (2, chips, piece, hidden)
        turns = ((0, soon), (0, late), (1, soon))
        weight_grad = write(where, turns, [kept_a, kept_b, other_a], shape)
        weight_grad = write(where, ((1, late),), [other_b], shape, weight_grad)
        return (activations, weight_grad.reshape(width, hidden))

    return local


def solution(mesh):
    return jax.shard_map(
        make_local(mesh.shape["row"], mesh.shape["col"]),
        mesh=mesh,
        in_specs=(
            P(("row", "col"), None),
            P(),
            P("row", "col", None, None, None, None),
            P("row", "col", None, None),
            P("row", "col", None),
            P(("row", "col"), None),
        ),
        out_specs=(P(("row", "col"), None), P()),
        check_vma=False,
    )
```

```python
import functools

import jax
import jax.numpy as jnp
from jax import lax
from jax.experimental import pallas as pl
from jax.experimental.pallas import tpu as pltpu
from jax.sharding import PartitionSpec as P

LIMIT = 8 * 1024 * 1024
VMEM = pl.BlockSpec(memory_space=pltpu.VMEM)
SMEM = pl.BlockSpec(memory_space=pltpu.SMEM)
HBM = pl.BlockSpec(memory_space=pltpu.HBM)


def place_kernel(groups, ids_ref, col_ref, count_ref, tiles_ref, *out_refs):
    row_blocks, slots, block = tiles_ref.shape[2:5]
    rows = groups[-1][1] * 2
    chips = rows // 2
    for out_ref in out_refs:
        out_ref[...] = jnp.zeros_like(out_ref)
    for q in range(row_blocks):
        a = q ^ ids_ref[1]
        for k in range(slots):
            position = (col_ref[0, 0, a, k] ^ ids_ref[0]) & (rows - 1)
            slot = (chips - position // 2) % chips
            live = k < count_ref[0, 0, a]
            for (parity, last, first), out_ref in zip(groups, out_refs):
                here = (position % 2 == parity) & (slot >= first) & (slot < last)

                @pl.when(live & here)
                def _(out_ref=out_ref, first=first, q=q, k=k, a=a, slot=slot):
                    start = pl.multiple_of((slot - first) * block, block)
                    out_ref[pl.ds(q * block, block), pl.ds(start, block)] = tiles_ref[0, 0, a, k]


def placed(ids, tile_col, tile_count, edge_tiles, chips):
    row_blocks, _, block = edge_tiles.shape[2:5]
    early = chips // 2
    groups = ((0, early, 0), (1, early, 0), (0, chips, early), (1, chips, early))
    held = 4 * edge_tiles.size + 8 * row_blocks * chips * block * block
    return pl.pallas_call(
        functools.partial(place_kernel, groups),
        out_shape=tuple(
            jax.ShapeDtypeStruct((row_blocks * block, (last - first) * block), jnp.bfloat16)
            for _, last, first in groups
        ),
        in_specs=[SMEM] * 3 + [VMEM],
        out_specs=(VMEM,) * 4,
        compiler_params=pltpu.CompilerParams(vmem_limit_bytes=max(LIMIT, held)),
        cost_estimate=pl.CostEstimate(
            flops=edge_tiles.size, bytes_accessed=6 * edge_tiles.size, transcendentals=0
        ),
    )(ids, tile_col, tile_count, edge_tiles)


def columns_of(ref, half, size):
    return ref[:, pl.ds(pl.multiple_of(half * size, size), size)]


def grad_half(agg_ref, pre_grad, half, size):
    return lax.dot_general(
        columns_of(agg_ref, half, size),
        pre_grad,
        (((0,), (0,)), ((), ())),
        preferred_element_type=jnp.float32,
    )


def dense_kernel(half_ref, *refs):
    parts, (weight_ref, cot_ref), (agg_ref, preact_ref, pre_ref, sent_ref) = (
        refs[:-6],
        refs[-6:-4],
        refs[-4:],
    )
    total = parts[0][...].astype(jnp.float32)
    for part in parts[1:]:
        total = total + part[...].astype(jnp.float32)
    agg_ref[...] = total.astype(jnp.bfloat16)
    preact = jnp.dot(agg_ref[...], weight_ref[...], preferred_element_type=jnp.float32)
    sigmoid = jax.nn.sigmoid(preact)
    preact_ref[...] = preact
    pre_ref[...] = (
        cot_ref[...].astype(jnp.float32) * sigmoid * (1.0 + preact * (1.0 - sigmoid))
    ).astype(jnp.bfloat16)
    size = sent_ref.shape[0]
    sent_ref[...] = grad_half(agg_ref, pre_ref[...], 1 - half_ref[0], size).astype(jnp.bfloat16)


def kept_kernel(half_ref, agg_ref, pre_ref, preact_ref, kept_ref, act_ref):
    preact = preact_ref[...]
    act_ref[...] = (preact * jax.nn.sigmoid(preact)).astype(jnp.bfloat16)
    kept_ref[...] = grad_half(agg_ref, pre_ref[...], half_ref[0], kept_ref.shape[0])


def write_kernel(turns, half_ref, own_ref, other_ref, *refs):
    sources, (out_ref, wide_ref, sems) = refs[: len(turns)], refs[-3:]
    size = wide_ref.shape[1]
    copies = []
    for (flip, partners), source in zip(turns, sources):
        half = 1 - half_ref[0] if flip else half_ref[0]
        place = other_ref[0] if flip else own_ref[0]
        for i, k in enumerate(partners):
            n = len(copies)
            wide_ref[n] = source[pl.ds(i * size, size), :].astype(jnp.float32)
            target = out_ref.at[half, place ^ k]
            copies.append(pltpu.make_async_copy(wide_ref.at[n], target, sems.at[n]))
            copies[-1].start()
    for copy in copies:
        copy.wait()


def write(where, turns, sources, shape, out=None):
    size, hidden = shape[2:]
    total = sum(len(partners) for _, partners in turns)
    earlier = [] if out is None else [out]
    return pl.pallas_call(
        functools.partial(write_kernel, turns),
        out_shape=jax.ShapeDtypeStruct(shape, jnp.float32),
        in_specs=[SMEM] * 3 + [VMEM] * len(sources) + [HBM] * len(earlier),
        out_specs=HBM,
        scratch_shapes=[
            pltpu.VMEM((total, size, hidden), jnp.float32),
            pltpu.SemaphoreType.DMA((total,)),
        ],
        input_output_aliases={3 + len(sources): 0} if earlier else {},
        compiler_params=pltpu.CompilerParams(vmem_limit_bytes=LIMIT),
        cost_estimate=pl.CostEstimate(
            flops=total * size * hidden, bytes_accessed=6 * total * size * hidden, transcendentals=0
        ),
    )(*where, *sources, *earlier)


def dense_part(half, parts, weight, cotangent):
    block, width = parts[0].shape
    hidden = weight.shape[1]
    size = width // 2
    agg, preact, pre, sent = pl.pallas_call(
        dense_kernel,
        out_shape=(
            jax.ShapeDtypeStruct((block, width), jnp.bfloat16),
            jax.ShapeDtypeStruct((block, hidden), jnp.float32),
            jax.ShapeDtypeStruct((block, hidden), jnp.bfloat16),
            jax.ShapeDtypeStruct((size, hidden), jnp.bfloat16),
        ),
        in_specs=[SMEM] + [VMEM] * (len(parts) + 2),
        out_specs=(VMEM,) * 4,
        compiler_params=pltpu.CompilerParams(vmem_limit_bytes=LIMIT),
        cost_estimate=pl.CostEstimate(
            flops=3 * block * width * hidden, bytes_accessed=8 * block * width, transcendentals=0
        ),
    )(half, *parts, weight, cotangent)
    kept, act = pl.pallas_call(
        kept_kernel,
        out_shape=(
            jax.ShapeDtypeStruct((size, hidden), jnp.float32),
            jax.ShapeDtypeStruct((block, hidden), jnp.bfloat16),
        ),
        in_specs=[SMEM] + [VMEM] * 3,
        out_specs=(VMEM,) * 2,
        compiler_params=pltpu.CompilerParams(vmem_limit_bytes=LIMIT),
        cost_estimate=pl.CostEstimate(
            flops=block * width * hidden, bytes_accessed=4 * block * width, transcendentals=0
        ),
    )(half, agg, pre, preact)
    return act, sent, kept


def make_local(rows, cols):
    chips = rows // 2

    def over_row(value, bits):
        return lax.ppermute(value, "row", [(i, i ^ bits) for i in range(rows)])

    def over_col(value, bits):
        return lax.ppermute(value, "col", [(i, i ^ bits) for i in range(cols)])

    def by_core(value, bits, flip):
        pairs = []
        for i in range(rows):
            for j in range(cols):
                if i % 2 == flip:
                    target = (i ^ (2 * bits)) * cols + j
                else:
                    target = i * cols + (j ^ bits)
                pairs.append((i * cols + j, target))
        return lax.ppermute(value, ("row", "col"), pairs)

    def local(features, weight, edge_tiles, tile_col, tile_count, cotangent):
        block, width = features.shape
        my_row = lax.axis_index("row")
        my_col = lax.axis_index("col")
        chip = my_row // 2

        far = [over_row(features, 2 * k) for k in range(chips - 1, 0, -1)]
        early = chips // 2
        even_a = jnp.concatenate([features] + far[: early - 1])
        odd_a = over_row(even_a, 1)
        even_b = jnp.concatenate(far[early - 1 :])
        odd_b = over_row(even_b, 1)

        ids = jnp.stack([my_row, my_col]).astype(jnp.int32)
        left = placed(ids, tile_col, tile_count, edge_tiles, chips)

        def product(one, other):
            return jnp.dot(one, other, preferred_element_type=jnp.float32)

        near_part = product(left[0], even_a) + product(left[1], odd_a) + product(left[2], even_b)

        def term(k):
            at = slice(k * block, (k + 1) * block)
            return (near_part[at] + product(left[3][at], odd_b)).astype(jnp.bfloat16)

        turns = sorted(range(1, cols), key=lambda k: (k != cols - 1, k))
        got = [over_col(term(k), k) for k in turns]

        half = (my_row % 2).astype(jnp.int32)
        activations, sent, kept = dense_part(half[None], [term(0)] + got, weight, cotangent)

        size, hidden = sent.shape
        kept = kept + over_row(sent, 1).astype(jnp.float32)
        if chips == cols:
            place = jnp.where(my_row % 2 == 0, chip, my_col)
            place_other = jnp.where(my_row % 2 == 0, my_col, chip)
            first = lambda value, k: by_core(value, k, 0)
            second = lambda value, k: by_core(value, k, 1)
        else:
            place = place_other = chip
            first = lambda value, k: over_row(value, 2 * k)
            second = over_col
        piece = size // chips
        kept = kept.reshape(chips, piece, hidden)
        mine = lax.dynamic_index_in_dim(kept, place, 0, keepdims=False)
        for k in [1] + list(range(chips - 1, 1, -1)):
            other = lax.dynamic_index_in_dim(kept, place ^ k, 0, keepdims=False)
            mine = mine + first(other.astype(jnp.bfloat16), k).astype(jnp.float32)
        mine = mine.astype(jnp.bfloat16)
        parts = [second(mine, k) for k in range(cols - 1, 0, -1)] + [mine]
        parts = [part.astype(jnp.float32) for part in parts]
        while len(parts) > 1:
            parts = [parts[i] + parts[i + 1] for i in range(0, len(parts), 2)]
        mine = parts[0].astype(jnp.bfloat16)
        gathered = [first(mine, k) for k in range(chips - 1, 0, -1)]
        soon = [0] + list(range(chips - 1, early, -1))
        late = list(range(early, 0, -1))
        kept_a = jnp.concatenate([mine] + gathered[: early - 1])
        other_a = over_row(kept_a, 1)
        kept_b = jnp.concatenate(gathered[early - 1 :])
        other_b = over_row(kept_b, 1)
        where = [value.astype(jnp.int32)[None] for value in (half, place, place_other)]
        shape = (2, chips, piece, hidden)
        turns = ((0, soon), (0, late), (1, soon))
        weight_grad = write(where, turns, [kept_a, kept_b, other_a], shape)
        weight_grad = write(where, ((1, late),), [other_b], shape, weight_grad)
        return (activations, weight_grad.reshape(width, hidden))

    return local


def solution(mesh):
    return jax.shard_map(
        make_local(mesh.shape["row"], mesh.shape["col"]),
        mesh=mesh,
        in_specs=(
            P(("row", "col"), None),
            P(),
            P("row", "col", None, None, None, None),
            P("row", "col", None, None),
            P("row", "col", None),
            P(("row", "col"), None),
        ),
        out_specs=(P(("row", "col"), None), P()),
        check_vma=False,
    )
```

```python
import functools

import jax
import jax.numpy as jnp
from jax import lax
from jax.experimental import pallas as pl
from jax.experimental.pallas import tpu as pltpu
from jax.sharding import PartitionSpec as P

LIMIT = 4 * 1024 * 1024
VMEM = pl.BlockSpec(memory_space=pltpu.VMEM)
SMEM = pl.BlockSpec(memory_space=pltpu.SMEM)
HBM = pl.BlockSpec(memory_space=pltpu.HBM)


def place_kernel(groups, row_ref, at_ref, col_ref, count_ref, tiles_ref, *out_refs):
    row_blocks, slots, block = tiles_ref.shape[2:5]
    rows = groups[-1][1] * 2
    chips = rows // 2
    for out_ref in out_refs:
        out_ref[...] = jnp.zeros_like(out_ref)
    for q in range(row_blocks):
        a = q ^ at_ref[0]
        for k in range(slots):
            position = (col_ref[0, 0, a, k] ^ row_ref[0]) & (rows - 1)
            slot = (chips - position // 2) % chips
            live = k < count_ref[0, 0, a]
            for (parity, last, first), out_ref in zip(groups, out_refs):
                here = (position % 2 == parity) & (slot >= first) & (slot < last)

                @pl.when(live & here)
                def _(out_ref=out_ref, first=first, q=q, k=k, a=a, slot=slot):
                    start = pl.multiple_of((slot - first) * block, block)
                    out_ref[pl.ds(q * block, block), pl.ds(start, block)] = tiles_ref[0, 0, a, k]


def placed(ids, tile_col, tile_count, edge_tiles, chips):
    row_blocks, _, block = edge_tiles.shape[2:5]
    early = chips // 2
    groups = ((0, early, 0), (1, early, 0), (0, chips, early), (1, chips, early))
    held = 4 * edge_tiles.size + 8 * row_blocks * chips * block * block
    return pl.pallas_call(
        functools.partial(place_kernel, groups),
        out_shape=tuple(
            jax.ShapeDtypeStruct((row_blocks * block, (last - first) * block), jnp.bfloat16)
            for _, last, first in groups
        ),
        in_specs=[SMEM] * 4 + [VMEM],
        out_specs=(VMEM,) * 4,
        compiler_params=pltpu.CompilerParams(vmem_limit_bytes=max(LIMIT, held)),
        cost_estimate=pl.CostEstimate(
            flops=edge_tiles.size, bytes_accessed=6 * edge_tiles.size, transcendentals=0
        ),
    )(*ids, tile_col, tile_count, edge_tiles)


def columns_of(ref, half, size):
    return ref[:, pl.ds(pl.multiple_of(half * size, size), size)]


def grad_half(agg_ref, pre_grad, half, size):
    return lax.dot_general(
        columns_of(agg_ref, half, size),
        pre_grad,
        (((0,), (0,)), ((), ())),
        preferred_element_type=jnp.float32,
    )


def dense_kernel(half_ref, *refs):
    parts, (weight_ref, cot_ref), (agg_ref, preact_ref, pre_ref, sent_ref) = (
        refs[:-6],
        refs[-6:-4],
        refs[-4:],
    )
    total = parts[0][...].astype(jnp.float32)
    for part in parts[1:]:
        total = total + part[...].astype(jnp.float32)
    agg_ref[...] = total.astype(jnp.bfloat16)
    preact = jnp.dot(agg_ref[...], weight_ref[...], preferred_element_type=jnp.float32)
    sigmoid = jax.nn.sigmoid(preact)
    preact_ref[...] = preact
    pre_ref[...] = (
        cot_ref[...].astype(jnp.float32) * sigmoid * (1.0 + preact * (1.0 - sigmoid))
    ).astype(jnp.bfloat16)
    size = sent_ref.shape[0]
    sent_ref[...] = grad_half(agg_ref, pre_ref[...], 1 - half_ref[0], size).astype(jnp.bfloat16)


def kept_kernel(half_ref, agg_ref, pre_ref, preact_ref, kept_ref, act_ref):
    preact = preact_ref[...]
    act_ref[...] = (preact * jax.nn.sigmoid(preact)).astype(jnp.bfloat16)
    kept_ref[...] = grad_half(agg_ref, pre_ref[...], half_ref[0], kept_ref.shape[0])


def write_kernel(turns, half_ref, own_ref, other_ref, *refs):
    sources, (out_ref, wide_ref, sems) = refs[: len(turns)], refs[-3:]
    size = wide_ref.shape[1]
    copies = []
    for (flip, partners), source in zip(turns, sources):
        half = 1 - half_ref[0] if flip else half_ref[0]
        place = other_ref[0] if flip else own_ref[0]
        for i, k in enumerate(partners):
            n = len(copies)
            wide_ref[n] = source[pl.ds(i * size, size), :].astype(jnp.float32)
            target = out_ref.at[half, place ^ k]
            copies.append(pltpu.make_async_copy(wide_ref.at[n], target, sems.at[n]))
            copies[-1].start()
    for copy in copies:
        copy.wait()


def write(where, turns, sources, shape, out=None):
    size, hidden = shape[2:]
    total = sum(len(partners) for _, partners in turns)
    earlier = [] if out is None else [out]
    return pl.pallas_call(
        functools.partial(write_kernel, turns),
        out_shape=jax.ShapeDtypeStruct(shape, jnp.float32),
        in_specs=[SMEM] * 3 + [VMEM] * len(sources) + [HBM] * len(earlier),
        out_specs=HBM,
        scratch_shapes=[
            pltpu.VMEM((total, size, hidden), jnp.float32),
            pltpu.SemaphoreType.DMA((total,)),
        ],
        input_output_aliases={3 + len(sources): 0} if earlier else {},
        compiler_params=pltpu.CompilerParams(vmem_limit_bytes=LIMIT),
        cost_estimate=pl.CostEstimate(
            flops=total * size * hidden, bytes_accessed=6 * total * size * hidden, transcendentals=0
        ),
    )(*where, *sources, *earlier)


def dense_part(half, parts, weight, cotangent):
    block, width = parts[0].shape
    hidden = weight.shape[1]
    size = width // 2
    agg, preact, pre, sent = pl.pallas_call(
        dense_kernel,
        out_shape=(
            jax.ShapeDtypeStruct((block, width), jnp.bfloat16),
            jax.ShapeDtypeStruct((block, hidden), jnp.float32),
            jax.ShapeDtypeStruct((block, hidden), jnp.bfloat16),
            jax.ShapeDtypeStruct((size, hidden), jnp.bfloat16),
        ),
        in_specs=[SMEM] + [VMEM] * (len(parts) + 2),
        out_specs=(VMEM,) * 4,
        compiler_params=pltpu.CompilerParams(vmem_limit_bytes=LIMIT),
        cost_estimate=pl.CostEstimate(
            flops=3 * block * width * hidden, bytes_accessed=8 * block * width, transcendentals=0
        ),
    )(half, *parts, weight, cotangent)
    kept, act = pl.pallas_call(
        kept_kernel,
        out_shape=(
            jax.ShapeDtypeStruct((size, hidden), jnp.float32),
            jax.ShapeDtypeStruct((block, hidden), jnp.bfloat16),
        ),
        in_specs=[SMEM] + [VMEM] * 3,
        out_specs=(VMEM,) * 2,
        compiler_params=pltpu.CompilerParams(vmem_limit_bytes=LIMIT),
        cost_estimate=pl.CostEstimate(
            flops=block * width * hidden, bytes_accessed=4 * block * width, transcendentals=0
        ),
    )(half, agg, pre, preact)
    return act, sent, kept


def make_local(rows, cols):
    chips = rows // 2

    def over_row(value, bits):
        return lax.ppermute(value, "row", [(i, i ^ bits) for i in range(rows)])

    def over_col(value, bits):
        return lax.ppermute(value, "col", [(i, i ^ bits) for i in range(cols)])

    def by_core(value, bits, flip):
        pairs = []
        for i in range(rows):
            for j in range(cols):
                if i % 2 == flip:
                    target = (i ^ (2 * bits)) * cols + j
                else:
                    target = i * cols + (j ^ bits)
                pairs.append((i * cols + j, target))
        return lax.ppermute(value, ("row", "col"), pairs)

    def local(features, weight, edge_tiles, tile_col, tile_count, cotangent):
        block, width = features.shape
        my_row = lax.axis_index("row")
        my_col = lax.axis_index("col")
        chip = my_row // 2

        far = [over_row(features, 2 * k) for k in range(chips - 1, 0, -1)]
        early = chips // 2
        even_a = jnp.concatenate([features] + far[: early - 1])
        odd_a = over_row(even_a, 1)
        even_b = jnp.concatenate(far[early - 1 :])
        odd_b = over_row(even_b, 1)

        ids = [value.astype(jnp.int32)[None] for value in (my_row, my_col)]
        left = placed(ids, tile_col, tile_count, edge_tiles, chips)

        def product(one, other):
            return jnp.dot(one, other, preferred_element_type=jnp.float32)

        near_part = product(left[0], even_a) + product(left[1], odd_a) + product(left[2], even_b)

        def term(k):
            at = slice(k * block, (k + 1) * block)
            return (near_part[at] + product(left[3][at], odd_b)).astype(jnp.bfloat16)

        turns = sorted(range(1, cols), key=lambda k: (k != cols - 1, k))
        got = [over_col(term(k), k) for k in turns]

        half = (my_row % 2).astype(jnp.int32)
        activations, sent, kept = dense_part(half[None], [term(0)] + got, weight, cotangent)

        size, hidden = sent.shape
        kept = kept + over_row(sent, 1).astype(jnp.float32)
        if chips == cols:
            place = jnp.where(my_row % 2 == 0, chip, my_col)
            place_other = jnp.where(my_row % 2 == 0, my_col, chip)
            first = lambda value, k: by_core(value, k, 0)
            second = lambda value, k: by_core(value, k, 1)
        else:
            place = place_other = chip
            first = lambda value, k: over_row(value, 2 * k)
            second = over_col
        piece = size // chips
        kept = kept.reshape(chips, piece, hidden)
        mine = lax.dynamic_index_in_dim(kept, place, 0, keepdims=False)
        for k in [1] + list(range(chips - 1, 1, -1)):
            other = lax.dynamic_index_in_dim(kept, place ^ k, 0, keepdims=False)
            mine = mine + first(other.astype(jnp.bfloat16), k).astype(jnp.float32)
        mine = mine.astype(jnp.bfloat16)
        parts = [second(mine, k) for k in range(cols - 1, 0, -1)] + [mine]
        parts = [part.astype(jnp.float32) for part in parts]
        while len(parts) > 1:
            parts = [parts[i] + parts[i + 1] for i in range(0, len(parts), 2)]
        mine = parts[0].astype(jnp.bfloat16)
        gathered = [first(mine, k) for k in range(chips - 1, 0, -1)]
        soon = [0] + list(range(chips - 1, early, -1))
        late = list(range(early, 0, -1))
        kept_a = jnp.concatenate([mine] + gathered[: early - 1])
        other_a = over_row(kept_a, 1)
        kept_b = jnp.concatenate(gathered[early - 1 :])
        other_b = over_row(kept_b, 1)
        where = [value.astype(jnp.int32)[None] for value in (half, place, place_other)]
        shape = (2, chips, piece, hidden)
        turns = ((0, soon), (0, late), (1, soon))
        weight_grad = write(where, turns, [kept_a, kept_b, other_a], shape)
        weight_grad = write(where, ((1, late),), [other_b], shape, weight_grad)
        return (activations, weight_grad.reshape(width, hidden))

    return local


def solution(mesh):
    return jax.shard_map(
        make_local(mesh.shape["row"], mesh.shape["col"]),
        mesh=mesh,
        in_specs=(
            P(("row", "col"), None),
            P(),
            P("row", "col", None, None, None, None),
            P("row", "col", None, None),
            P("row", "col", None),
            P(("row", "col"), None),
        ),
        out_specs=(P(("row", "col"), None), P()),
        check_vma=False,
    )
```
